32 devices in a mesh: dp: 4 (over y, x), tile: 8 (over z, core).
Axes of the slice: x: 2, y: 2, z: 4, core: 2. Of those that a mesh axis runs over, the one named last changes fastest.
Arguments:
- features: bfloat16 [4, 64, 64, 128], P('dp', None, 'tile'), may hold values from -6 to 6
- occupied_block_mask: int32 [4, 8, 2], P('dp', 'tile'), may hold values 0 or 1
- conv_one: bfloat16 [27, 64, 64], replicated, may hold values from -0.15625 to 0.15625
- conv_two: bfloat16 [27, 64, 64], replicated, may hold values from -0.15625 to 0.15625
- gain: float32 [64], replicated, may hold values from 0.5 to 1.5
- shift: float32 [64], replicated, may hold values from -3 to 3
- cotangent: bfloat16 [4, 64, 64, 128], P('dp', None, 'tile'), may hold values from -6 to 6
Outputs:
- section_out: bfloat16 [4, 64, 64, 128], P('dp', None, 'tile')
- input_grad: bfloat16 [4, 64, 64, 128], P('dp', None, 'tile')
- grad_one: float32 [27, 64, 64], replicated
- grad_two: float32 [27, 64, 64], replicated
- gain_grad: float32 [64], replicated
- shift_grad: float32 [64], replicated
The draws below stay inside these ranges and needn't reach their ends.
Inputs may be any that keep to these rules, and one draw needn't show every extreme that they name: `occupied_block_mask`: each entry marks whether a block holds points.
All inputs are finite; a program needn't handle non-finite values.
Results may differ from the reference program's by a relative error of at most 0.0034.
Values may be sent and summed in bfloat16 or wider, within the bound.
A program may use at most 128 MiB of HBM per device.

```python
import jax
import jax.numpy as jnp
from jax import lax

CH = 64
BLK = 8
TAPS = 27
YB = 2
SCENES = 4
NXB = 8
NX = 64
HY = 128


def touch_ends(array, rng, least, top_value):
    place = [jax.random.randint(jax.random.fold_in(rng, axis), (), 0, length) for axis, length in enumerate(array.shape)]
    main_axis = array.shape.index(max(array.shape))
    neighbour = place[:main_axis] + [(place[main_axis] + 1) % array.shape[main_axis]] + place[main_axis + 1:]
    return array.at[tuple(place)].set(least).at[tuple(neighbour)].set(top_value)


def steps_of(key, dims, shards, least, high):
    level = 1.0
    for position, shards_of in shards:
        steps = jax.random.uniform(jax.random.fold_in(jax.random.fold_in(key, 6), position), (shards_of,), jnp.float32, least / len(shards), high / len(shards))
        level = level * jnp.repeat(jnp.exp(steps), dims[position] // shards_of).reshape((-1,) + (1,) * (len(dims) - 1 - position))
    return level


def noise(rng, shape, width, limit, shards=(), dtype=jnp.bfloat16):
    drawn = width * jax.random.normal(rng, shape, jnp.float32)
    if shards:
        drawn = drawn * steps_of(rng, shape, shards, -0.22, 0.18)
    return jnp.clip(drawn, -limit, limit).astype(dtype)


def setup_inputs(seed: int = 0) -> dict:
    keys = jax.random.split(jax.random.key(seed), 8)
    features = noise(keys[0], (SCENES, CH, NX, HY), 1.0, 6.0, ((0, 4), (2, 8)))
    occupied_block_mask = touch_ends((jax.random.randint(keys[1], (SCENES, NXB, YB), 0, 4) < 3).astype(jnp.int32), jax.random.fold_in(keys[1], 1), 0, 1)
    conv_one = noise(keys[2], (TAPS, CH, CH), (TAPS * CH) ** -0.5, 0.15625)
    conv_two = noise(keys[3], (TAPS, CH, CH), (TAPS * CH) ** -0.5, 0.15625)
    gain = jnp.clip(1.0 + 0.1 * jax.random.normal(keys[4], (CH,), jnp.float32), 0.5, 1.5)
    shift = noise(keys[5], (CH,), 0.5, 3.0, (), jnp.float32)
    cotangent = noise(keys[6], (SCENES, CH, NX, HY), 1.0, 6.0, ((0, 4), (2, 8)))
    return {"features": features, "occupied_block_mask": occupied_block_mask, "conv_one": conv_one, "conv_two": conv_two, "gain": gain, "shift": shift, "cotangent": cotangent}


epsilon = 1e-05

def voxel_mask(occupied_block_mask, block_edge):
    scenes_here, x_blocks, y_blocks = occupied_block_mask.shape
    grown = jnp.broadcast_to(occupied_block_mask[:, :, None, None, :, None], (scenes_here, x_blocks, block_edge, block_edge, y_blocks, block_edge))
    return grown.reshape(scenes_here, 1, x_blocks * block_edge, block_edge * y_blocks * block_edge)

def widen(padded_x, height):
    scenes_here, channels, x_size, flat_size = padded_x.shape
    shaped = padded_x.reshape(scenes_here, channels, x_size, height, flat_size // height)
    return jnp.pad(shaped, ((0, 0), (0, 0), (0, 0), (1, 1), (1, 1)))

def window_rows(padded_grid, offset_x, offset_h):
    scenes_here, channels, x_pad, h_pad, y_pad = padded_grid.shape
    x_span, h_span, y_span = (x_pad - 2, h_pad - 2, y_pad - 2)
    pieces = [padded_grid[:, :, offset_x:offset_x + x_span, offset_h:offset_h + h_span, offset_y:offset_y + y_span] for offset_y in range(3)]
    return jnp.concatenate(pieces, axis=1).reshape(scenes_here, 3 * channels, x_span * h_span * y_span)

def convolve_one(padded_grid, weight):
    running = None
    for offset_x in range(3):
        for offset_h in range(3):
            column_matrix = window_rows(padded_grid, offset_x, offset_h).astype(jnp.float32)
            kernel_tap_block = weight[9 * offset_x + 3 * offset_h:9 * offset_x + 3 * offset_h + 3].reshape(-1, weight.shape[2]).astype(jnp.float32)
            matrix_product = jnp.einsum('zl,pzh->plh', kernel_tap_block, column_matrix, precision=lax.Precision.HIGHEST)
            running = matrix_product if running is None else running + matrix_product
    return running

def kernel_grad_one(padded_grid, delta_row_matrix):
    pieces = []
    for offset_x in range(3):
        for offset_h in range(3):
            column_matrix = window_rows(padded_grid, offset_x, offset_h).astype(jnp.float32)
            matrix_product = jnp.einsum('uzh,uih->zi', column_matrix, delta_row_matrix.astype(jnp.float32), precision=lax.Precision.HIGHEST)
            pieces.append(matrix_product.reshape(3, -1, matrix_product.shape[1]))
    return jnp.concatenate(pieces, axis=0)

def flipped(weight):
    return jnp.transpose(weight[::-1], (0, 2, 1))

def convolve_all(padded_grid, weight, shape_out):
    result = lax.map(lambda one_grid: convolve_one(one_grid[None], weight)[0], padded_grid)
    return result.reshape(shape_out)

def kernel_gradient_total(padded_grid, delta_row_matrix):
    per_scene = lax.map(lambda pair: kernel_grad_one(pair[0][None], pair[1][None]), (padded_grid, delta_row_matrix))
    return lax.optimization_barrier(jnp.sum(per_scene, axis=0))

def pad_x(array_in):
    return jnp.pad(array_in, ((0, 0), (0, 0), (1, 1), (0, 0)))

def reference(features, occupied_block_mask, conv_one, conv_two, gain, shift, cotangent):
    shape_out = features.shape
    scenes_all, channels = (shape_out[0], shape_out[1])
    vox_mask = voxel_mask(occupied_block_mask, BLK).astype(jnp.bfloat16)
    mask_f = vox_mask.astype(jnp.float32)
    inputs = features * vox_mask
    x_grid = widen(pad_x(inputs), BLK)
    pre_one = convolve_all(x_grid, conv_one, shape_out)
    active_count = jnp.sum(mask_f) * 1.0
    bn_mean = lax.optimization_barrier(jnp.sum(pre_one * mask_f, axis=(0, 2, 3))) / active_count
    centered = (pre_one - bn_mean[None, :, None, None]) * mask_f
    variance = lax.optimization_barrier(jnp.sum(centered * centered, axis=(0, 2, 3))) / active_count
    inv_std = lax.rsqrt(variance + epsilon)
    normal = (pre_one - bn_mean[None, :, None, None]) * inv_std[None, :, None, None]
    pre_act = gain[None, :, None, None] * normal + shift[None, :, None, None]
    act = (jax.nn.silu(pre_act) * mask_f).astype(jnp.bfloat16)
    a_grid = widen(pad_x(act), BLK)
    pre_two = convolve_all(a_grid, conv_two, shape_out)
    section_out = ((inputs.astype(jnp.float32) + pre_two) * mask_f).astype(jnp.bfloat16)
    delta_out = cotangent * vox_mask
    grad_two = kernel_gradient_total(a_grid, delta_out.reshape(scenes_all, channels, -1))
    d_grid = widen(pad_x(delta_out), BLK)
    activation_gradient = convolve_all(d_grid, flipped(conv_two), shape_out)
    sigmoid_z = jax.nn.sigmoid(pre_act)
    z_grad = activation_gradient * mask_f * sigmoid_z * (1.0 + pre_act * (1.0 - sigmoid_z))
    shift_grad = lax.optimization_barrier(jnp.sum(z_grad, axis=(0, 2, 3)))
    gain_grad = lax.optimization_barrier(jnp.sum(z_grad * normal, axis=(0, 2, 3)))
    scale_c = (gain * inv_std)[None, :, None, None]
    first_delta_gradient = (scale_c * (z_grad - (shift_grad / active_count)[None, :, None, None] - normal * (gain_grad / active_count)[None, :, None, None]) * mask_f).astype(jnp.bfloat16)
    grad_one = kernel_gradient_total(x_grid, first_delta_gradient.reshape(scenes_all, channels, -1))
    i_grid = widen(pad_x(first_delta_gradient), BLK)
    back_in = convolve_all(i_grid, flipped(conv_one), shape_out)
    input_grad = ((delta_out.astype(jnp.float32) + back_in) * mask_f).astype(jnp.bfloat16)
    return (section_out, input_grad, grad_one, grad_two, gain_grad, shift_grad)
```

```python
import functools

import jax
import jax.numpy as jnp
from jax import lax
from jax.experimental import pallas as pl
from jax.experimental.pallas import tpu as pltpu
from jax.sharding import PartitionSpec as P

BLK = 8
LANES = 128
EPSILON = 1e-05
MESH = pl.DeviceIdType.MESH
F32 = jnp.float32
BF16 = jnp.bfloat16


def kernel(
    n_dp, n_tile, ch, nx, hy,
    xd_ref, mask_ref, w1_ref, w2_ref, w1f_ref, w2f_ref, gs_ref,
    so_ref, ig_ref, g1_ref, g2_ref, gain_out, shift_out,
    xd_pad, a_pad, i_pad, s_x, s_t, d3, ar_a, ar_b, part, r1, acc, r2, q3, q4,
    halo_s, halo_r, ar_s, ar_r, rs_s, rs_r,
):
    n_a, n_b = 2 * n_dp, n_tile // 2
    dp, tile = lax.axis_index("dp"), lax.axis_index("tile")
    core, z = lax.rem(tile, 2), tile // 2
    a_me = dp * 2 + core
    flat = nx * hy
    c_a = part.shape[1] // n_a
    c_b = c_a // n_b

    def peer_a(k):
        other = lax.rem(a_me + k, n_a)
        return other, (other // 2, z * 2 + lax.rem(other, 2))

    def peer_b(k):
        other = lax.rem(z + k, n_b)
        return other, (dp, other * 2 + core)

    has_left, has_right = tile > 0, tile < n_tile - 1

    barrier = pltpu.get_barrier_semaphore()
    for k in range(1, n_a):
        pl.semaphore_signal(barrier, inc=1, device_id=peer_a(k)[1], device_id_type=MESH)
    for k in range(1, n_b):
        pl.semaphore_signal(barrier, inc=1, device_id=peer_b(k)[1], device_id_type=MESH)

    @pl.when(has_left)
    def _():
        pl.semaphore_signal(barrier, inc=1, device_id=(dp, tile - 1), device_id_type=MESH)

    @pl.when(has_right)
    def _():
        pl.semaphore_signal(barrier, inc=1, device_id=(dp, tile + 1), device_id_type=MESH)

    sides = has_left.astype(jnp.int32) + has_right.astype(jnp.int32)
    pl.semaphore_wait(barrier, n_a + n_b - 2 + sides)

    def halo(phase, src, first, pad):
        low = pltpu.make_async_remote_copy(
            src_ref=src.at[:, pl.ds(first, hy)],
            dst_ref=pad.at[:, pl.ds(flat + hy, hy)],
            send_sem=halo_s.at[phase, 0], recv_sem=halo_r.at[phase, 0],
            device_id=(dp, tile - 1), device_id_type=MESH)
        high = pltpu.make_async_remote_copy(
            src_ref=src.at[:, pl.ds(first + flat - hy, hy)],
            dst_ref=pad.at[:, pl.ds(0, hy)],
            send_sem=halo_s.at[phase, 1], recv_sem=halo_r.at[phase, 1],
            device_id=(dp, tile + 1), device_id_type=MESH)

        @pl.when(has_left)
        def _():
            low.start()

        @pl.when(has_right)
        def _():
            high.start()

        def finish():
            @pl.when(has_left)
            def _():
                low.wait_send()
                high.wait_recv()

            @pl.when(has_right)
            def _():
                high.wait_send()
                low.wait_recv()

        return finish

    def zero_ends(pad):
        @pl.when(jnp.logical_not(has_left))
        def _():
            pad[:, pl.ds(0, hy)] = jnp.zeros((pad.shape[0], hy), pad.dtype)

        @pl.when(jnp.logical_not(has_right))
        def _():
            pad[:, pl.ds(flat + hy, hy)] = jnp.zeros((pad.shape[0], hy), pad.dtype)

    width = hy // BLK
    lane = lax.broadcasted_iota(jnp.int32, (1, hy), 1)
    row_h, row_y = lane // width, lax.rem(lane, width)

    def shifts(pad, first, out):
        def plane(x, carry):
            at = pl.ds(pl.multiple_of(x * hy, hy), hy)
            values = pad[pl.ds(first, ch), at].astype(F32)
            for b in range(3):
                for c in range(3):
                    step = (b - 1) * width + (c - 1)
                    moved = values
                    if step:
                        moved = pltpu.roll(values, (-step) % hy, 1)
                        fits = ((row_h + (b - 1) >= 0) & (row_h + (b - 1) < BLK)
                                & (row_y + (c - 1) >= 0) & (row_y + (c - 1) < width))
                        moved = jnp.where(fits, moved, 0.0)
                    out[pl.ds((3 * b + c) * ch, ch), at] = moved.astype(BF16)
            return carry
        lax.fori_loop(0, nx + 2, plane, 0)

    def conv(weight, stack):
        grown = jnp.dot(weight[...], stack[...], preferred_element_type=F32)
        return (grown[:ch, :flat] + grown[ch:2 * ch, hy:hy + flat]
                + grown[2 * ch:, 2 * hy:2 * hy + flat])

    def kernel_grad(stack, g):
        dims = (((1,), (1,)), ((), ()))
        rows = 9 * ch
        half = rows // 2
        part[g, pl.ds(0, rows), :] = lax.dot_general(
            stack[...], d3[pl.ds(0, 2 * ch), :], dims, preferred_element_type=F32)
        rest = lax.dot_general(
            stack[...], d3[pl.ds(2 * ch, ch), :], dims, preferred_element_type=F32)
        part[g, pl.ds(rows, half), :] = jnp.concatenate([rest[:half], rest[half:]], axis=1)

    def put_d3(value):
        for a in range(3):
            d3[pl.ds(a * ch, ch), pl.ds(a * hy, flat)] = value

    def to_rows(columns):
        spot = lax.broadcasted_iota(jnp.int32, (ch, LANES), 1)
        block = jnp.zeros((ch, LANES), F32)
        for index, column in enumerate(columns):
            block = jnp.where(spot == index, column, block)
        return jnp.transpose(block)[:8]

    def to_columns(rows):
        return jnp.transpose(jnp.concatenate([rows, jnp.zeros((LANES - 8, ch), F32)], axis=0))

    def spread(call, slots, mine, peers, size, base):
        copies = []
        for k in range(1, size):
            copy = pltpu.make_async_remote_copy(
                src_ref=slots.at[call, mine], dst_ref=slots.at[call, mine],
                send_sem=ar_s.at[call, base + k], recv_sem=ar_r.at[call, base + k],
                device_id=peers(k)[1], device_id_type=MESH)
            copy.start()
            copies.append(copy)
        return copies

    def wait_all(copies):
        for copy in copies:
            copy.wait()

    def small_start(call, rows):
        ar_a[call, a_me] = rows
        return spread(call, ar_a, a_me, peer_a, n_a, 0)

    def small_next(call, copies, merge):
        wait_all(copies)
        ar_b[call, z] = merge([ar_a[call, k] for k in range(n_a)])
        return spread(call, ar_b, z, peer_b, n_b, n_a)

    def small_end(call, copies, merge):
        wait_all(copies)
        return merge([ar_b[call, k] for k in range(n_b)])

    def add(rows):
        total = rows[0]
        for row in rows[1:]:
            total = total + row
        return total

    def merge_moments(rows):
        total = add(rows)
        count, sums = total[2:3], total[0:1]
        mean = sums / jnp.maximum(count, 1.0)
        spread_all = total[1:2]
        for row in rows:
            off = row[0:1] / jnp.maximum(row[2:3], 1.0) - mean
            spread_all = spread_all + row[2:3] * off * off
        return jnp.concatenate([sums, spread_all, count, jnp.zeros((5, ch), F32)], axis=0)

    def scatter_a(g):
        copies = []
        for k in range(1, n_a):
            other, device = peer_a(k)
            copy = pltpu.make_async_remote_copy(
                src_ref=part.at[g, pl.ds(pl.multiple_of(other * c_a, c_a), c_a), :],
                dst_ref=r1.at[g, k - 1],
                send_sem=rs_s.at[g, k], recv_sem=rs_r.at[g, k],
                device_id=device, device_id_type=MESH)
            copy.start()
            copies.append(copy)
        return copies

    def scatter_b(g, copies):
        wait_all(copies)
        total = part[g, pl.ds(pl.multiple_of(a_me * c_a, c_a), c_a), :]
        for k in range(1, n_a):
            total = total + r1[g, k - 1]
        acc[g] = total
        copies = []
        for k in range(1, n_b):
            other, device = peer_b(k)
            copy = pltpu.make_async_remote_copy(
                src_ref=acc.at[g, pl.ds(pl.multiple_of(other * c_b, c_b), c_b), :],
                dst_ref=r2.at[g, k - 1],
                send_sem=rs_s.at[g, n_a + k], recv_sem=rs_r.at[g, n_a + k],
                device_id=device, device_id_type=MESH)
            copy.start()
            copies.append(copy)
        return copies

    def gather_b(g, copies):
        wait_all(copies)
        mine = pl.ds(pl.multiple_of(z * c_b, c_b), c_b)
        total = acc[g, mine, :]
        for k in range(1, n_b):
            total = total + r2[g, k - 1]
        q3[g, mine, :] = total.astype(BF16)
        copies = []
        for k in range(1, n_b):
            copy = pltpu.make_async_remote_copy(
                src_ref=q3.at[g, mine, :], dst_ref=q3.at[g, mine, :],
                send_sem=rs_s.at[g, n_a + n_b + k], recv_sem=rs_r.at[g, n_a + n_b + k],
                device_id=peer_b(k)[1], device_id_type=MESH)
            copy.start()
            copies.append(copy)
        return copies

    def gather_a(g, copies):
        wait_all(copies)
        mine = pl.ds(pl.multiple_of(a_me * c_a, c_a), c_a)
        copies = []
        for k in range(1, n_a):
            copy = pltpu.make_async_remote_copy(
                src_ref=q3.at[g], dst_ref=q4.at[g, mine, :],
                send_sem=rs_s.at[g, n_a + 2 * n_b + k], recv_sem=rs_r.at[g, n_a + 2 * n_b + k],
                device_id=peer_a(k)[1], device_id_type=MESH)
            copy.start()
            copies.append(copy)
        q4[g, mine, :] = q3[g]
        return copies

    def write_grad(g, copies, out):
        wait_all(copies)
        rows = 9 * ch
        half = rows // 2
        for a in range(2):
            out[pl.ds(a * rows, rows), :] = q4[g, pl.ds(0, rows), pl.ds(a * ch, ch)].astype(F32)
        for side in range(2):
            out[pl.ds(2 * rows + side * half, half), :] = (
                q4[g, pl.ds(rows, half), pl.ds(side * ch, ch)].astype(F32))

    mask = mask_ref[...]
    end_xd = halo(0, xd_ref, 0, xd_pad)
    xd_pad[:, pl.ds(hy, flat)] = xd_ref[...]
    zero_ends(xd_pad)
    zero_ends(a_pad)
    zero_ends(i_pad)
    d3[...] = jnp.zeros(d3.shape, d3.dtype)
    put_d3(xd_ref[pl.ds(ch, ch), :])
    used = 27 * ch // 2
    for g in range(2):
        part[g, pl.ds(used, part.shape[1] - used), :] = jnp.zeros(
            (part.shape[1] - used, LANES), F32)
    end_xd()

    shifts(xd_pad, 0, s_x)
    pre = conv(w1_ref, s_x)
    count_here = jnp.sum(mask, axis=1, keepdims=True)
    sums_here = jnp.sum(pre * mask, axis=1, keepdims=True)
    off = (pre - sums_here / jnp.maximum(count_here, 1.0)) * mask
    squares_here = jnp.sum(off * off, axis=1, keepdims=True)
    copies = small_start(0, to_rows([sums_here, squares_here, count_here]))

    shifts(xd_pad, ch, s_t)
    act_grad = conv(w2f_ref, s_t)

    copies = small_next(0, copies, merge_moments)
    moments = to_columns(small_end(0, copies, merge_moments))
    count = moments[:, 2:3]
    mean = moments[:, 0:1] / count
    inv_std = lax.rsqrt(moments[:, 1:2] / count + EPSILON)
    gain, shift = gs_ref[:, 0:1], gs_ref[:, 1:2]
    normal = (pre - mean) * inv_std
    pre_act = gain * normal + shift
    sg = 1.0 / (1.0 + jnp.exp(-pre_act))
    a_pad[:, pl.ds(hy, flat)] = (pre_act * sg * mask).astype(BF16)
    end_act = halo(1, a_pad, hy, a_pad)
    z_grad = act_grad * mask * sg * (1.0 + pre_act * (1.0 - sg))
    shift_here = jnp.sum(z_grad, axis=1, keepdims=True)
    gain_here = jnp.sum(z_grad * normal, axis=1, keepdims=True)
    copies = small_start(1, to_rows([shift_here, gain_here]))

    end_act()
    shifts(a_pad, 0, s_t)
    copies = small_next(1, copies, add)
    kernel_grad(s_t, 0)
    totals = small_end(1, copies, add)
    shift_out[...] = totals[0:1]
    gain_out[...] = totals[1:2]
    totals = to_columns(totals)
    delta_one = (gain * inv_std * (
        z_grad - totals[:, 0:1] / count - normal * (totals[:, 1:2] / count)) * mask).astype(BF16)
    i_pad[:, pl.ds(hy, flat)] = delta_one
    end_delta = halo(2, i_pad, hy, i_pad)
    put_d3(delta_one)
    kernel_grad(s_x, 1)
    one = scatter_a(1)
    two = scatter_a(0)
    pre_two = conv(w2_ref, s_t)
    so_ref[...] = ((xd_ref[pl.ds(0, ch), :].astype(F32) + pre_two) * mask).astype(BF16)
    one = scatter_b(1, one)
    end_delta()
    shifts(i_pad, 0, s_t)
    two = scatter_b(0, two)
    one = gather_b(1, one)
    back = conv(w1f_ref, s_t)
    ig_ref[...] = ((xd_ref[pl.ds(ch, ch), :].astype(F32) + back) * mask).astype(BF16)
    two = gather_b(0, two)
    one = gather_a(1, one)
    two = gather_a(0, two)
    write_grad(1, one, g1_ref)
    write_grad(0, two, g2_ref)


def flat_kernel(taps):
    count, inner, outer = taps.shape
    return taps.reshape(3, count // 3 * inner, outer).transpose(0, 2, 1).reshape(3 * outer, -1)


def flat_flipped(taps):
    count, outer, inner = taps.shape
    return (taps[::-1].reshape(3, count // 3, outer, inner).transpose(0, 2, 1, 3)
            .reshape(3 * outer, -1))


def local(n_dp, n_tile, features, occupied, conv_one, conv_two, gain, shift, cotangent):
    scenes, ch, nx, hy = features.shape
    flat = nx * hy
    grown = jnp.broadcast_to(
        occupied[:, :, None, None, :, None],
        (1, nx // BLK, BLK, BLK, occupied.shape[2], BLK)).reshape(1, flat)
    mask = grown.astype(BF16)
    xd = jnp.concatenate(
        [features.reshape(ch, flat), cotangent.reshape(ch, flat)], axis=0) * mask
    n_a, n_b = 2 * n_dp, n_tile // 2
    c_b = -(-(27 * ch // 2) // (n_a * n_b * 16)) * 16
    c_a = c_b * n_b
    rows = c_a * n_a
    vmem = pl.BlockSpec(memory_space=pltpu.VMEM)
    dma = pltpu.SemaphoreType.DMA
    so, ig, g1, g2, gg, sg = pl.pallas_call(
        functools.partial(kernel, n_dp, n_tile, ch, nx, hy),
        out_shape=(
            jax.ShapeDtypeStruct((ch, flat), BF16),
            jax.ShapeDtypeStruct((ch, flat), BF16),
            jax.ShapeDtypeStruct((27 * ch, ch), F32),
            jax.ShapeDtypeStruct((27 * ch, ch), F32),
            jax.ShapeDtypeStruct((1, ch), F32),
            jax.ShapeDtypeStruct((1, ch), F32),
        ),
        in_specs=[vmem] * 7,
        out_specs=[vmem] * 6,
        scratch_shapes=[
            pltpu.VMEM((2 * ch, flat + 2 * hy), BF16),
            pltpu.VMEM((ch, flat + 2 * hy), BF16),
            pltpu.VMEM((ch, flat + 2 * hy), BF16),
            pltpu.VMEM((9 * ch, flat + 2 * hy), BF16),
            pltpu.VMEM((9 * ch, flat + 2 * hy), BF16),
            pltpu.VMEM((3 * ch, flat + 2 * hy), BF16),
            pltpu.VMEM((2, n_a, 8, ch), F32),
            pltpu.VMEM((2, n_b, 8, ch), F32),
            pltpu.VMEM((2, rows, LANES), F32),
            pltpu.VMEM((2, n_a - 1, c_a, LANES), F32),
            pltpu.VMEM((2, c_a, LANES), F32),
            pltpu.VMEM((2, n_b - 1, c_b, LANES), F32),
            pltpu.VMEM((2, c_a, LANES), BF16),
            pltpu.VMEM((2, rows, LANES), BF16),
            dma((3, 2)), dma((3, 2)),
            dma((2, n_a + n_b)), dma((2, n_a + n_b)),
            dma((2, 2 * (n_a + n_b))), dma((2, 2 * (n_a + n_b))),
        ],
        compiler_params=pltpu.CompilerParams(
            collective_id=0, has_side_effects=True, vmem_limit_bytes=48 * 2**20),
    )(
        xd, mask.astype(F32), flat_kernel(conv_one), flat_kernel(conv_two),
        flat_flipped(conv_one), flat_flipped(conv_two), jnp.stack([gain, shift], axis=1),
    )
    shape = features.shape
    return (so.reshape(shape), ig.reshape(shape), g1.reshape(27, ch, ch),
            g2.reshape(27, ch, ch), gg.reshape(ch), sg.reshape(ch))


def solution(mesh):
    split = P("dp", None, "tile", None)
    return jax.shard_map(
        functools.partial(local, mesh.shape["dp"], mesh.shape["tile"]),
        mesh=mesh,
        in_specs=(split, P("dp", "tile", None), P(), P(), P(), P(), split),
        out_specs=(split, split, P(), P(), P(), P()),
        check_vma=False,
    )
```

```python
import functools

import jax
import jax.numpy as jnp
from jax import lax
from jax.experimental import pallas as pl
from jax.experimental.pallas import tpu as pltpu
from jax.sharding import PartitionSpec as P

BLK = 8
LANES = 128
EPSILON = 1e-05
MESH = pl.DeviceIdType.MESH
F32 = jnp.float32
BF16 = jnp.bfloat16


def kernel(
    n_dp, n_tile, ch, nx, hy,
    xd_ref, occ_ref, k1_ref, k2_ref, gain_ref, shift_ref,
    so_ref, ig_ref, q4, sums_out,
    w1_ref, w2_ref, w1f_ref, w2f_ref, xd_pad, a_pad, i_pad, s_x, s_t, d3, ar_a, ar_b, part, r1, acc, r2, q3,
    halo_s, halo_r, ar_s, ar_r, rs_s, rs_r,
):
    n_a, n_b = 2 * n_dp, n_tile // 2
    dp, tile = lax.axis_index("dp"), lax.axis_index("tile")
    core, z = lax.rem(tile, 2), tile // 2
    a_me = dp * 2 + core
    flat = nx * hy
    c_a = part.shape[1] // n_a
    c_b = c_a // n_b

    def peer_a(k):
        other = lax.rem(a_me + k, n_a)
        return other, (other // 2, z * 2 + lax.rem(other, 2))

    def peer_b(k):
        other = lax.rem(z + k, n_b)
        return other, (dp, other * 2 + core)

    has_left, has_right = tile > 0, tile < n_tile - 1

    barrier = pltpu.get_barrier_semaphore()
    for k in range(1, n_a):
        pl.semaphore_signal(barrier, inc=1, device_id=peer_a(k)[1], device_id_type=MESH)
    for k in range(1, n_b):
        pl.semaphore_signal(barrier, inc=1, device_id=peer_b(k)[1], device_id_type=MESH)

    @pl.when(has_left)
    def _():
        pl.semaphore_signal(barrier, inc=1, device_id=(dp, tile - 1), device_id_type=MESH)

    @pl.when(has_right)
    def _():
        pl.semaphore_signal(barrier, inc=1, device_id=(dp, tile + 1), device_id_type=MESH)

    width = hy // BLK
    spot = lax.broadcasted_iota(jnp.int32, (1, flat), 1)
    block_x, block_y = spot // (hy * BLK), lax.rem(spot, width) // BLK
    mask = jnp.zeros((1, flat), F32)
    for bx in range(nx // BLK):
        for by in range(width // BLK):
            mask = jnp.where((block_x == bx) & (block_y == by),
                             occ_ref[bx, by].astype(F32), mask)
    xd_pad[:, pl.ds(hy, flat)] = (xd_ref[...].astype(F32) * mask).astype(BF16)
    same = (lax.broadcasted_iota(jnp.int32, (ch, ch), 0)
            == lax.broadcasted_iota(jnp.int32, (ch, ch), 1)).astype(BF16)

    def as_matrix(taps, out):
        for a in range(3):
            out[pl.ds(a * ch, ch), :] = lax.dot_general(
                same, taps[pl.ds(a * 9 * ch, 9 * ch), :], (((1,), (1,)), ((), ())),
                preferred_element_type=F32).astype(BF16)

    def as_flipped(taps, out):
        for a in range(3):
            out[pl.ds(a * ch, ch), :] = jnp.concatenate(
                [taps[pl.ds((26 - 9 * a - k) * ch, ch), :] for k in range(9)], axis=1)

    as_matrix(k1_ref, w1_ref)

    sides = has_left.astype(jnp.int32) + has_right.astype(jnp.int32)
    pl.semaphore_wait(barrier, n_a + n_b - 2 + sides)

    def halo(phase, src, first, pad):
        low = pltpu.make_async_remote_copy(
            src_ref=src.at[:, pl.ds(first, hy)],
            dst_ref=pad.at[:, pl.ds(flat + hy, hy)],
            send_sem=halo_s.at[phase, 0], recv_sem=halo_r.at[phase, 0],
            device_id=(dp, tile - 1), device_id_type=MESH)
        high = pltpu.make_async_remote_copy(
            src_ref=src.at[:, pl.ds(first + flat - hy, hy)],
            dst_ref=pad.at[:, pl.ds(0, hy)],
            send_sem=halo_s.at[phase, 1], recv_sem=halo_r.at[phase, 1],
            device_id=(dp, tile + 1), device_id_type=MESH)

        @pl.when(has_left)
        def _():
            low.start()

        @pl.when(has_right)
        def _():
            high.start()

        def finish():
            @pl.when(has_left)
            def _():
                low.wait_send()
                high.wait_recv()

            @pl.when(has_right)
            def _():
                high.wait_send()
                low.wait_recv()

        return finish

    def zero_ends(pad):
        @pl.when(jnp.logical_not(has_left))
        def _():
            pad[:, pl.ds(0, hy)] = jnp.zeros((pad.shape[0], hy), pad.dtype)

        @pl.when(jnp.logical_not(has_right))
        def _():
            pad[:, pl.ds(flat + hy, hy)] = jnp.zeros((pad.shape[0], hy), pad.dtype)

    lane = lax.broadcasted_iota(jnp.int32, (1, hy), 1)
    row_h, row_y = lane // width, lax.rem(lane, width)

    def shifts(pad, first, out):
        def plane(x, carry):
            at = pl.ds(pl.multiple_of(x * hy, hy), hy)
            values = pad[pl.ds(first, ch), at]
            for b in range(3):
                for c in range(3):
                    step = (b - 1) * width + (c - 1)
                    moved = values
                    if step:
                        moved = pltpu.roll(values, (-step) % hy, 1)
                        fits = ((row_h + (b - 1) >= 0) & (row_h + (b - 1) < BLK)
                                & (row_y + (c - 1) >= 0) & (row_y + (c - 1) < width))
                        moved = jnp.where(fits, moved, jnp.zeros_like(moved))
                    out[pl.ds((3 * b + c) * ch, ch), at] = moved.astype(BF16)
            return carry
        lax.fori_loop(0, nx + 2, plane, 0, unroll=True)

    def conv(weight, stack):
        grown = jnp.dot(weight[...], stack[...], preferred_element_type=F32)
        return (grown[:ch, :flat] + grown[ch:2 * ch, hy:hy + flat]
                + grown[2 * ch:, 2 * hy:2 * hy + flat])

    def kernel_grad(stack, g):
        dims = (((1,), (1,)), ((), ()))
        rows = 9 * ch
        half = rows // 2
        part[g, pl.ds(0, rows), :] = lax.dot_general(
            stack[...], d3[pl.ds(0, 2 * ch), :], dims, preferred_element_type=F32)
        rest = lax.dot_general(
            stack[...], d3[pl.ds(2 * ch, ch), :], dims, preferred_element_type=F32)
        part[g, pl.ds(rows, half), :] = jnp.concatenate([rest[:half], rest[half:]], axis=1)

    def put_d3(value):
        for a in range(3):
            d3[pl.ds(a * ch, ch), pl.ds(a * hy, flat)] = value

    def to_rows(columns):
        spot = lax.broadcasted_iota(jnp.int32, (ch, LANES), 1)
        block = jnp.zeros((ch, LANES), F32)
        for index, column in enumerate(columns):
            block = jnp.where(spot == index, column, block)
        return jnp.transpose(block)[:8]

    def to_columns(rows):
        return jnp.transpose(jnp.concatenate([rows, jnp.zeros((LANES - 8, ch), F32)], axis=0))

    def spread(call, slots, mine, peers, size, base):
        copies = []
        for k in range(1, size):
            copy = pltpu.make_async_remote_copy(
                src_ref=slots.at[call, mine], dst_ref=slots.at[call, mine],
                send_sem=ar_s.at[call, base + k], recv_sem=ar_r.at[call, base + k],
                device_id=peers(k)[1], device_id_type=MESH)
            copy.start()
            copies.append(copy)
        return copies

    def wait_all(copies):
        for copy in copies:
            copy.wait()

    def small_start(call, rows):
        ar_a[call, a_me] = rows
        return spread(call, ar_a, a_me, peer_a, n_a, 0)

    def small_next(call, copies, merge):
        wait_all(copies)
        ar_b[call, z] = merge([ar_a[call, k] for k in range(n_a)])
        return spread(call, ar_b, z, peer_b, n_b, n_a)

    def small_end(call, copies, merge):
        wait_all(copies)
        return merge([ar_b[call, k] for k in range(n_b)])

    def add(rows):
        total = rows[0]
        for row in rows[1:]:
            total = total + row
        return total

    def merge_moments(rows):
        total = add(rows)
        count, sums = total[2:3], total[0:1]
        mean = sums / jnp.maximum(count, 1.0)
        spread_all = total[1:2]
        for row in rows:
            off = row[0:1] / jnp.maximum(row[2:3], 1.0) - mean
            spread_all = spread_all + row[2:3] * off * off
        return jnp.concatenate([sums, spread_all, count, jnp.zeros((5, ch), F32)], axis=0)

    def scatter_a(g):
        copies = []
        for k in range(1, n_a):
            other, device = peer_a(k)
            copy = pltpu.make_async_remote_copy(
                src_ref=part.at[g, pl.ds(pl.multiple_of(other * c_a, c_a), c_a), :],
                dst_ref=r1.at[g, k - 1],
                send_sem=rs_s.at[g, k], recv_sem=rs_r.at[g, k],
                device_id=device, device_id_type=MESH)
            copy.start()
            copies.append(copy)
        return copies

    def scatter_b(g, copies):
        wait_all(copies)
        total = part[g, pl.ds(pl.multiple_of(a_me * c_a, c_a), c_a), :]
        for k in range(1, n_a):
            total = total + r1[g, k - 1]
        acc[g] = total
        copies = []
        for k in range(1, n_b):
            other, device = peer_b(k)
            copy = pltpu.make_async_remote_copy(
                src_ref=acc.at[g, pl.ds(pl.multiple_of(other * c_b, c_b), c_b), :],
                dst_ref=r2.at[g, k - 1],
                send_sem=rs_s.at[g, n_a + k], recv_sem=rs_r.at[g, n_a + k],
                device_id=device, device_id_type=MESH)
            copy.start()
            copies.append(copy)
        return copies

    def gather_b(g, copies):
        wait_all(copies)
        mine = pl.ds(pl.multiple_of(z * c_b, c_b), c_b)
        total = acc[g, mine, :]
        for k in range(1, n_b):
            total = total + r2[g, k - 1]
        q3[g, mine, :] = total.astype(BF16)
        copies = []
        for k in range(1, n_b):
            copy = pltpu.make_async_remote_copy(
                src_ref=q3.at[g, mine, :], dst_ref=q3.at[g, mine, :],
                send_sem=rs_s.at[g, n_a + n_b + k], recv_sem=rs_r.at[g, n_a + n_b + k],
                device_id=peer_b(k)[1], device_id_type=MESH)
            copy.start()
            copies.append(copy)
        return copies

    def gather_a(g, copies):
        wait_all(copies)
        mine = pl.ds(pl.multiple_of(a_me * c_a, c_a), c_a)
        copies = []
        for k in range(1, n_a):
            copy = pltpu.make_async_remote_copy(
                src_ref=q3.at[g], dst_ref=q4.at[g, mine, :],
                send_sem=rs_s.at[g, n_a + 2 * n_b + k], recv_sem=rs_r.at[g, n_a + 2 * n_b + k],
                device_id=peer_a(k)[1], device_id_type=MESH)
            copy.start()
            copies.append(copy)
        q4[g, mine, :] = q3[g]
        return copies

    end_xd = halo(0, xd_pad, hy, xd_pad)
    as_flipped(k2_ref, w2f_ref)
    as_matrix(k2_ref, w2_ref)
    as_flipped(k1_ref, w1f_ref)
    gain_shift = to_columns(jnp.concatenate(
        [gain_ref[...], shift_ref[...], jnp.zeros((6, ch), F32)], axis=0))
    zero_ends(xd_pad)
    zero_ends(a_pad)
    zero_ends(i_pad)
    d3[...] = jnp.zeros(d3.shape, d3.dtype)
    put_d3(xd_pad[pl.ds(ch, ch), pl.ds(hy, flat)])
    used = 27 * ch // 2
    for g in range(2):
        part[g, pl.ds(used, part.shape[1] - used), :] = jnp.zeros(
            (part.shape[1] - used, LANES), F32)
    end_xd()

    shifts(xd_pad, 0, s_x)
    pre = conv(w1_ref, s_x)
    count_here = jnp.sum(mask, axis=1, keepdims=True)
    sums_here = jnp.sum(pre * mask, axis=1, keepdims=True)
    off = (pre - sums_here / jnp.maximum(count_here, 1.0)) * mask
    squares_here = jnp.sum(off * off, axis=1, keepdims=True)
    copies = small_start(0, to_rows([sums_here, squares_here, count_here]))

    shifts(xd_pad, ch, s_t)
    act_grad = conv(w2f_ref, s_t)

    copies = small_next(0, copies, merge_moments)
    moments = to_columns(small_end(0, copies, merge_moments))
    count = moments[:, 2:3]
    mean = moments[:, 0:1] / count
    inv_std = lax.rsqrt(moments[:, 1:2] / count + EPSILON)
    gain, shift = gain_shift[:, 0:1], gain_shift[:, 1:2]
    normal = (pre - mean) * inv_std
    pre_act = gain * normal + shift
    sg = 1.0 / (1.0 + jnp.exp(-pre_act))
    a_pad[:, pl.ds(hy, flat)] = (pre_act * sg * mask).astype(BF16)
    end_act = halo(1, a_pad, hy, a_pad)
    z_grad = act_grad * mask * sg * (1.0 + pre_act * (1.0 - sg))
    shift_here = jnp.sum(z_grad, axis=1, keepdims=True)
    gain_here = jnp.sum(z_grad * normal, axis=1, keepdims=True)
    copies = small_start(1, to_rows([shift_here, gain_here]))

    end_act()
    shifts(a_pad, 0, s_t)
    copies = small_next(1, copies, add)
    kernel_grad(s_t, 0)
    totals = small_end(1, copies, add)
    sums_out[...] = totals
    totals = to_columns(totals)
    delta_one = (gain * inv_std * (
        z_grad - totals[:, 0:1] / count - normal * (totals[:, 1:2] / count)) * mask).astype(BF16)
    i_pad[:, pl.ds(hy, flat)] = delta_one
    end_delta = halo(2, i_pad, hy, i_pad)
    put_d3(delta_one)
    kernel_grad(s_x, 1)
    one = scatter_a(1)
    two = scatter_a(0)
    pre_two = conv(w2_ref, s_t)
    so_ref[...] = ((xd_pad[pl.ds(0, ch), pl.ds(hy, flat)].astype(F32) + pre_two) * mask).astype(BF16)
    one = scatter_b(1, one)
    end_delta()
    shifts(i_pad, 0, s_t)
    two = scatter_b(0, two)
    one = gather_b(1, one)
    back = conv(w1f_ref, s_t)
    ig_ref[...] = ((xd_pad[pl.ds(ch, ch), pl.ds(hy, flat)].astype(F32) + back) * mask).astype(BF16)
    two = gather_b(0, two)
    one = gather_a(1, one)
    two = gather_a(0, two)
    wait_all(one)
    wait_all(two)


def unpack(ch, so_in, ig_in, q4, sums, so_ref, ig_ref, g1_ref, g2_ref, gain_ref, shift_ref):
    rows = 9 * ch
    half = rows // 2
    for g, out in ((1, g1_ref), (0, g2_ref)):
        for a in range(2):
            out[pl.ds(a * rows, rows), :] = q4[g, pl.ds(0, rows), pl.ds(a * ch, ch)].astype(F32)
        for side in range(2):
            out[pl.ds(2 * rows + side * half, half), :] = (
                q4[g, pl.ds(rows, half), pl.ds(side * ch, ch)].astype(F32))
    so_ref[...] = so_in[...]
    ig_ref[...] = ig_in[...]
    shift_ref[...] = sums[0:1, :]
    gain_ref[...] = sums[1:2, :]


def local(n_dp, n_tile, features, occupied, conv_one, conv_two, gain, shift, cotangent):
    scenes, ch, nx, hy = features.shape
    flat = nx * hy
    xd = jnp.concatenate([features.reshape(ch, flat), cotangent.reshape(ch, flat)], axis=0)
    n_a, n_b = 2 * n_dp, n_tile // 2
    c_b = -(-(27 * ch // 2) // (n_a * n_b * 16)) * 16
    c_a = c_b * n_b
    rows = c_a * n_a
    vmem = pl.BlockSpec(memory_space=pltpu.VMEM)
    dma = pltpu.SemaphoreType.DMA
    so, ig, q4, sums = pl.pallas_call(
        functools.partial(kernel, n_dp, n_tile, ch, nx, hy),
        out_shape=(
            jax.ShapeDtypeStruct((ch, flat), BF16),
            jax.ShapeDtypeStruct((ch, flat), BF16),
            jax.ShapeDtypeStruct((2, rows, LANES), BF16),
            jax.ShapeDtypeStruct((8, ch), F32),
        ),
        in_specs=[vmem, pl.BlockSpec(memory_space=pltpu.SMEM)] + [vmem] * 4,
        out_specs=[vmem] * 4,
        scratch_shapes=[
            pltpu.VMEM((3 * ch, 9 * ch), BF16),
            pltpu.VMEM((3 * ch, 9 * ch), BF16),
            pltpu.VMEM((3 * ch, 9 * ch), BF16),
            pltpu.VMEM((3 * ch, 9 * ch), BF16),
            pltpu.VMEM((2 * ch, flat + 2 * hy), BF16),
            pltpu.VMEM((ch, flat + 2 * hy), BF16),
            pltpu.VMEM((ch, flat + 2 * hy), BF16),
            pltpu.VMEM((9 * ch, flat + 2 * hy), BF16),
            pltpu.VMEM((9 * ch, flat + 2 * hy), BF16),
            pltpu.VMEM((3 * ch, flat + 2 * hy), BF16),
            pltpu.VMEM((2, n_a, 8, ch), F32),
            pltpu.VMEM((2, n_b, 8, ch), F32),
            pltpu.VMEM((2, rows, LANES), F32),
            pltpu.VMEM((2, n_a - 1, c_a, LANES), F32),
            pltpu.VMEM((2, c_a, LANES), F32),
            pltpu.VMEM((2, n_b - 1, c_b, LANES), F32),
            pltpu.VMEM((2, c_a, LANES), BF16),
            dma((3, 2)), dma((3, 2)),
            dma((2, n_a + n_b)), dma((2, n_a + n_b)),
            dma((2, 2 * (n_a + n_b))), dma((2, 2 * (n_a + n_b))),
        ],
        compiler_params=pltpu.CompilerParams(
            collective_id=0, has_side_effects=True, vmem_limit_bytes=48 * 2**20),
    )(
        xd, occupied[0], conv_one.reshape(27 * ch, ch), conv_two.reshape(27 * ch, ch),
        gain.reshape(1, ch), shift.reshape(1, ch),
    )
    planes = features.shape[1:]
    so, ig, g1, g2, gg, sg = pl.pallas_call(
        functools.partial(unpack, ch),
        out_shape=(
            jax.ShapeDtypeStruct(planes, BF16),
            jax.ShapeDtypeStruct(planes, BF16),
            jax.ShapeDtypeStruct((27 * ch, ch), F32),
            jax.ShapeDtypeStruct((27 * ch, ch), F32),
            jax.ShapeDtypeStruct((1, ch), F32),
            jax.ShapeDtypeStruct((1, ch), F32),
        ),
        in_specs=[vmem] * 4,
        out_specs=[vmem] * 6,
        compiler_params=pltpu.CompilerParams(vmem_limit_bytes=16 * 2**20),
    )(so.reshape(planes), ig.reshape(planes), q4, sums)
    shape = features.shape
    return (so.reshape(shape), ig.reshape(shape), g1.reshape(27, ch, ch),
            g2.reshape(27, ch, ch), gg.reshape(ch), sg.reshape(ch))


def solution(mesh):
    split = P("dp", None, "tile", None)
    return jax.shard_map(
        functools.partial(local, mesh.shape["dp"], mesh.shape["tile"]),
        mesh=mesh,
        in_specs=(split, P("dp", "tile", None), P(), P(), P(), P(), split),
        out_specs=(split, split, P(), P(), P(), P()),
        check_vma=False,
    )
```

```python
import functools

import jax
import jax.numpy as jnp
from jax import lax
from jax.experimental import pallas as pl
from jax.experimental.pallas import tpu as pltpu
from jax.sharding import PartitionSpec as P

BLK = 8
LANES = 128
EPSILON = 1e-05
MESH = pl.DeviceIdType.MESH
F32 = jnp.float32
BF16 = jnp.bfloat16


def kernel(
    n_dp, n_tile, ch, nx, hy,
    xd_ref, occ_ref, k1_ref, k2_ref, gain_ref, shift_ref,
    so_ref, ig_ref, q4, sums_out,
    w1_ref, w2_ref, w1f_ref, w2f_ref, xd_pad, a_pad, i_pad, s_x, s_t, d3, ar_a, ar_b, part, rp, half_sum, r1, acc, r2, q3,
    halo_s, halo_r, ar_s, ar_r, rs_s, rs_r,
):
    n_a, n_b = 2 * n_dp, n_tile // 2
    dp, tile = lax.axis_index("dp"), lax.axis_index("tile")
    core, z = lax.rem(tile, 2), tile // 2
    a_me = core * n_dp + dp
    flat = nx * hy
    c_a = part.shape[1] // n_a
    c_b = c_a // n_b

    def peer_a(k):
        other = lax.rem(a_me + k, n_a)
        return other, (lax.rem(other, n_dp), z * 2 + other // n_dp)

    def peer_b(k):
        other = lax.rem(z + k, n_b)
        return other, (dp, other * 2 + core)

    has_left, has_right = tile > 0, tile < n_tile - 1

    barrier = pltpu.get_barrier_semaphore()
    for k in range(1, n_a):
        pl.semaphore_signal(barrier, inc=1, device_id=peer_a(k)[1], device_id_type=MESH)
    for k in range(1, n_b):
        pl.semaphore_signal(barrier, inc=1, device_id=peer_b(k)[1], device_id_type=MESH)

    @pl.when(has_left)
    def _():
        pl.semaphore_signal(barrier, inc=1, device_id=(dp, tile - 1), device_id_type=MESH)

    @pl.when(has_right)
    def _():
        pl.semaphore_signal(barrier, inc=1, device_id=(dp, tile + 1), device_id_type=MESH)

    width = hy // BLK
    spot = lax.broadcasted_iota(jnp.int32, (1, flat), 1)
    block_x, block_y = spot // (hy * BLK), lax.rem(spot, width) // BLK
    mask = jnp.zeros((1, flat), F32)
    for bx in range(nx // BLK):
        for by in range(width // BLK):
            mask = jnp.where((block_x == bx) & (block_y == by),
                             occ_ref[bx, by].astype(F32), mask)
    xd_pad[:, pl.ds(hy, flat)] = (xd_ref[...].astype(F32) * mask).astype(BF16)
    same = (lax.broadcasted_iota(jnp.int32, (ch, ch), 0)
            == lax.broadcasted_iota(jnp.int32, (ch, ch), 1)).astype(BF16)

    def as_matrix(taps, out):
        for a in range(3):
            out[pl.ds(a * ch, ch), :] = lax.dot_general(
                same, taps[pl.ds(a * 9 * ch, 9 * ch), :], (((1,), (1,)), ((), ())),
                preferred_element_type=F32).astype(BF16)

    def as_flipped(taps, out):
        for a in range(3):
            out[pl.ds(a * ch, ch), :] = jnp.concatenate(
                [taps[pl.ds((26 - 9 * a - k) * ch, ch), :] for k in range(9)], axis=1)

    as_matrix(k1_ref, w1_ref)

    sides = has_left.astype(jnp.int32) + has_right.astype(jnp.int32)
    pl.semaphore_wait(barrier, n_a + n_b - 2 + sides)

    def halo(phase, src, first, pad):
        low = pltpu.make_async_remote_copy(
            src_ref=src.at[:, pl.ds(first, hy)],
            dst_ref=pad.at[:, pl.ds(flat + hy, hy)],
            send_sem=halo_s.at[phase, 0], recv_sem=halo_r.at[phase, 0],
            device_id=(dp, tile - 1), device_id_type=MESH)
        high = pltpu.make_async_remote_copy(
            src_ref=src.at[:, pl.ds(first + flat - hy, hy)],
            dst_ref=pad.at[:, pl.ds(0, hy)],
            send_sem=halo_s.at[phase, 1], recv_sem=halo_r.at[phase, 1],
            device_id=(dp, tile + 1), device_id_type=MESH)

        @pl.when(has_left)
        def _():
            low.start()

        @pl.when(has_right)
        def _():
            high.start()

        def finish():
            @pl.when(has_left)
            def _():
                low.wait_send()
                high.wait_recv()

            @pl.when(has_right)
            def _():
                high.wait_send()
                low.wait_recv()

        return finish

    def zero_ends(pad):
        @pl.when(jnp.logical_not(has_left))
        def _():
            pad[:, pl.ds(0, hy)] = jnp.zeros((pad.shape[0], hy), pad.dtype)

        @pl.when(jnp.logical_not(has_right))
        def _():
            pad[:, pl.ds(flat + hy, hy)] = jnp.zeros((pad.shape[0], hy), pad.dtype)

    lane = lax.broadcasted_iota(jnp.int32, (1, hy), 1)
    row_h, row_y = lane // width, lax.rem(lane, width)

    def shifts(pad, first, out, inner=True, outer=True):
        def plane(x, carry):
            at = pl.ds(x * hy if isinstance(x, int) else pl.multiple_of(x * hy, hy), hy)
            values = pad[pl.ds(first, ch), at]
            for b in range(3):
                for c in range(3):
                    step = (b - 1) * width + (c - 1)
                    moved = values
                    if step:
                        moved = pltpu.roll(values, (-step) % hy, 1)
                        fits = ((row_h + (b - 1) >= 0) & (row_h + (b - 1) < BLK)
                                & (row_y + (c - 1) >= 0) & (row_y + (c - 1) < width))
                        moved = jnp.where(fits, moved, jnp.zeros_like(moved))
                    out[pl.ds((3 * b + c) * ch, ch), at] = moved.astype(BF16)
            return carry
        if inner:
            lax.fori_loop(1, nx + 1, plane, 0, unroll=True)
        if outer:
            plane(0, 0)
            plane(nx + 1, 0)

    def conv(weight, stack):
        grown = jnp.dot(weight[...], stack[...], preferred_element_type=F32)
        return (grown[:ch, :flat] + grown[ch:2 * ch, hy:hy + flat]
                + grown[2 * ch:, 2 * hy:2 * hy + flat])

    def kernel_grad(stack, g):
        dims = (((1,), (1,)), ((), ()))
        rows = 9 * ch
        half = rows // 2
        part[g, pl.ds(0, rows), :] = lax.dot_general(
            stack[...], d3[pl.ds(0, 2 * ch), :], dims, preferred_element_type=F32)
        rest = lax.dot_general(
            stack[...], d3[pl.ds(2 * ch, ch), :], dims, preferred_element_type=F32)
        part[g, pl.ds(rows, half), :] = jnp.concatenate([rest[:half], rest[half:]], axis=1)

    def put_d3(value):
        for a in range(3):
            d3[pl.ds(a * ch, ch), pl.ds(a * hy, flat)] = value

    def to_rows(columns):
        spot = lax.broadcasted_iota(jnp.int32, (ch, LANES), 1)
        block = jnp.zeros((ch, LANES), F32)
        for index, column in enumerate(columns):
            block = jnp.where(spot == index, column, block)
        return jnp.transpose(block)[:8]

    def to_columns(rows):
        return jnp.transpose(jnp.concatenate([rows, jnp.zeros((LANES - 8, ch), F32)], axis=0))

    def spread(call, slots, mine, peers, size, base):
        copies = []
        for k in range(1, size):
            copy = pltpu.make_async_remote_copy(
                src_ref=slots.at[call, mine], dst_ref=slots.at[call, mine],
                send_sem=ar_s.at[call, base + k], recv_sem=ar_r.at[call, base + k],
                device_id=peers(k)[1], device_id_type=MESH)
            copy.start()
            copies.append(copy)
        return copies

    def wait_all(copies):
        for copy in copies:
            copy.wait()

    def small_start(call, rows):
        ar_a[call, a_me] = rows
        return spread(call, ar_a, a_me, peer_a, n_a, 0)

    def small_next(call, copies, merge):
        wait_all(copies)
        ar_b[call, z] = merge([ar_a[call, k] for k in range(n_a)])
        return spread(call, ar_b, z, peer_b, n_b, n_a)

    def small_end(call, copies, merge):
        wait_all(copies)
        return merge([ar_b[call, k] for k in range(n_b)])

    def add(rows):
        total = rows[0]
        for row in rows[1:]:
            total = total + row
        return total

    def merge_moments(rows):
        total = add(rows)
        count, sums = total[2:3], total[0:1]
        mean = sums / jnp.maximum(count, 1.0)
        spread_all = total[1:2]
        for row in rows:
            off = row[0:1] / jnp.maximum(row[2:3], 1.0) - mean
            spread_all = spread_all + row[2:3] * off * off
        return jnp.concatenate([sums, spread_all, count, jnp.zeros((5, ch), F32)], axis=0)

    half_rows = part.shape[1] // 2

    def scatter_core(g):
        theirs = pl.ds(pl.multiple_of((1 - core) * half_rows, half_rows), half_rows)
        copy = pltpu.make_async_remote_copy(
            src_ref=part.at[g, theirs, :], dst_ref=rp.at[g],
            send_sem=rs_s.at[g, 0], recv_sem=rs_r.at[g, 0],
            device_id=(dp, z * 2 + 1 - core), device_id_type=MESH)
        copy.start()
        return [copy]

    def scatter_a(g, copies):
        wait_all(copies)
        mine = pl.ds(pl.multiple_of(core * half_rows, half_rows), half_rows)
        half_sum[g] = part[g, mine, :] + rp[g]
        copies = []
        for k in range(1, n_dp):
            other = lax.rem(dp + k, n_dp)
            copy = pltpu.make_async_remote_copy(
                src_ref=half_sum.at[g, pl.ds(pl.multiple_of(other * c_a, c_a), c_a), :],
                dst_ref=r1.at[g, k - 1],
                send_sem=rs_s.at[g, k], recv_sem=rs_r.at[g, k],
                device_id=(other, tile), device_id_type=MESH)
            copy.start()
            copies.append(copy)
        return copies

    def scatter_b(g, copies):
        wait_all(copies)
        total = half_sum[g, pl.ds(pl.multiple_of(dp * c_a, c_a), c_a), :]
        for k in range(1, n_dp):
            total = total + r1[g, k - 1]
        acc[g] = total
        copies = []
        for k in range(1, n_b):
            other, device = peer_b(k)
            copy = pltpu.make_async_remote_copy(
                src_ref=acc.at[g, pl.ds(pl.multiple_of(other * c_b, c_b), c_b), :],
                dst_ref=r2.at[g, k - 1],
                send_sem=rs_s.at[g, n_a + k], recv_sem=rs_r.at[g, n_a + k],
                device_id=device, device_id_type=MESH)
            copy.start()
            copies.append(copy)
        return copies

    def gather_b(g, copies):
        wait_all(copies)
        mine = pl.ds(pl.multiple_of(z * c_b, c_b), c_b)
        total = acc[g, mine, :]
        for k in range(1, n_b):
            total = total + r2[g, k - 1]
        q3[g, mine, :] = total.astype(BF16)
        copies = []
        for k in range(1, n_b):
            copy = pltpu.make_async_remote_copy(
                src_ref=q3.at[g, mine, :], dst_ref=q3.at[g, mine, :],
                send_sem=rs_s.at[g, n_a + n_b + k], recv_sem=rs_r.at[g, n_a + n_b + k],
                device_id=peer_b(k)[1], device_id_type=MESH)
            copy.start()
            copies.append(copy)
        return copies

    def gather_a(g, copies):
        wait_all(copies)
        mine = pl.ds(pl.multiple_of(a_me * c_a, c_a), c_a)
        copies = []
        for k in range(1, n_a):
            copy = pltpu.make_async_remote_copy(
                src_ref=q3.at[g], dst_ref=q4.at[g, mine, :],
                send_sem=rs_s.at[g, n_a + 2 * n_b + k], recv_sem=rs_r.at[g, n_a + 2 * n_b + k],
                device_id=peer_a(k)[1], device_id_type=MESH)
            copy.start()
            copies.append(copy)
        q4[g, mine, :] = q3[g]
        return copies

    end_xd = halo(0, xd_pad, hy, xd_pad)
    shifts(xd_pad, 0, s_x, outer=False)
    zero_ends(xd_pad)
    zero_ends(a_pad)
    zero_ends(i_pad)
    end_xd()

    shifts(xd_pad, 0, s_x, inner=False)
    pre = conv(w1_ref, s_x)
    count_here = jnp.sum(mask, axis=1, keepdims=True)
    sums_here = jnp.sum(pre * mask, axis=1, keepdims=True)
    off = (pre - sums_here / jnp.maximum(count_here, 1.0)) * mask
    squares_here = jnp.sum(off * off, axis=1, keepdims=True)
    copies = small_start(0, to_rows([sums_here, squares_here, count_here]))

    shifts(xd_pad, ch, s_t)
    as_flipped(k2_ref, w2f_ref)
    act_grad = conv(w2f_ref, s_t)
    gain_shift = to_columns(jnp.concatenate(
        [gain_ref[...], shift_ref[...], jnp.zeros((6, ch), F32)], axis=0))

    copies = small_next(0, copies, merge_moments)
    d3[...] = jnp.zeros(d3.shape, d3.dtype)
    put_d3(xd_pad[pl.ds(ch, ch), pl.ds(hy, flat)])
    used = 27 * ch // 2
    for g in range(2):
        part[g, pl.ds(used, part.shape[1] - used), :] = jnp.zeros(
            (part.shape[1] - used, LANES), F32)
    moments = to_columns(small_end(0, copies, merge_moments))
    count = moments[:, 2:3]
    mean = moments[:, 0:1] / count
    inv_std = lax.rsqrt(moments[:, 1:2] / count + EPSILON)
    gain, shift = gain_shift[:, 0:1], gain_shift[:, 1:2]
    normal = (pre - mean) * inv_std
    pre_act = gain * normal + shift
    sg = 1.0 / (1.0 + jnp.exp(-pre_act))
    a_pad[:, pl.ds(hy, flat)] = (pre_act * sg * mask).astype(BF16)
    end_act = halo(1, a_pad, hy, a_pad)
    z_grad = act_grad * mask * sg * (1.0 + pre_act * (1.0 - sg))
    shift_here = jnp.sum(z_grad, axis=1, keepdims=True)
    gain_here = jnp.sum(z_grad * normal, axis=1, keepdims=True)
    copies = small_start(1, to_rows([shift_here, gain_here]))

    as_matrix(k2_ref, w2_ref)
    as_flipped(k1_ref, w1f_ref)
    shifts(a_pad, 0, s_t, outer=False)
    end_act()
    shifts(a_pad, 0, s_t, inner=False)
    copies = small_next(1, copies, add)
    kernel_grad(s_t, 0)
    two = scatter_core(0)
    totals = small_end(1, copies, add)
    sums_out[...] = totals
    totals = to_columns(totals)
    delta_one = (gain * inv_std * (
        z_grad - totals[:, 0:1] / count - normal * (totals[:, 1:2] / count)) * mask).astype(BF16)
    i_pad[:, pl.ds(hy, flat)] = delta_one
    end_delta = halo(2, i_pad, hy, i_pad)
    put_d3(delta_one)
    kernel_grad(s_x, 1)
    one = scatter_core(1)
    two = scatter_a(0, two)
    pre_two = conv(w2_ref, s_t)
    so_ref[...] = ((xd_pad[pl.ds(0, ch), pl.ds(hy, flat)].astype(F32) + pre_two) * mask).astype(BF16)
    one = scatter_a(1, one)
    two = scatter_b(0, two)
    shifts(i_pad, 0, s_t, outer=False)
    end_delta()
    shifts(i_pad, 0, s_t, inner=False)
    one = scatter_b(1, one)
    two = gather_b(0, two)
    back = conv(w1f_ref, s_t)
    ig_ref[...] = ((xd_pad[pl.ds(ch, ch), pl.ds(hy, flat)].astype(F32) + back) * mask).astype(BF16)
    one = gather_b(1, one)
    two = gather_a(0, two)
    one = gather_a(1, one)
    wait_all(one)
    wait_all(two)


def unpack(ch, so_in, ig_in, q4, sums, so_ref, ig_ref, g1_ref, g2_ref, gain_ref, shift_ref):
    rows = 9 * ch
    half = rows // 2
    for g, out in ((1, g1_ref), (0, g2_ref)):
        for a in range(2):
            out[pl.ds(a * rows, rows), :] = q4[g, pl.ds(0, rows), pl.ds(a * ch, ch)].astype(F32)
        for side in range(2):
            out[pl.ds(2 * rows + side * half, half), :] = (
                q4[g, pl.ds(rows, half), pl.ds(side * ch, ch)].astype(F32))
    so_ref[...] = so_in[...]
    ig_ref[...] = ig_in[...]
    shift_ref[...] = sums[0:1, :]
    gain_ref[...] = sums[1:2, :]


def local(n_dp, n_tile, features, occupied, conv_one, conv_two, gain, shift, cotangent):
    scenes, ch, nx, hy = features.shape
    flat = nx * hy
    xd = jnp.concatenate([features.reshape(ch, flat), cotangent.reshape(ch, flat)], axis=0)
    n_a, n_b = 2 * n_dp, n_tile // 2
    c_b = -(-(27 * ch // 2) // (n_a * n_b * 16)) * 16
    c_a = c_b * n_b
    rows = c_a * n_a
    vmem = pl.BlockSpec(memory_space=pltpu.VMEM)
    dma = pltpu.SemaphoreType.DMA
    so, ig, q4, sums = pl.pallas_call(
        functools.partial(kernel, n_dp, n_tile, ch, nx, hy),
        out_shape=(
            jax.ShapeDtypeStruct((ch, flat), BF16),
            jax.ShapeDtypeStruct((ch, flat), BF16),
            jax.ShapeDtypeStruct((2, rows, LANES), BF16),
            jax.ShapeDtypeStruct((8, ch), F32),
        ),
        in_specs=[vmem, pl.BlockSpec(memory_space=pltpu.SMEM)] + [vmem] * 4,
        out_specs=[vmem] * 4,
        scratch_shapes=[
            pltpu.VMEM((3 * ch, 9 * ch), BF16),
            pltpu.VMEM((3 * ch, 9 * ch), BF16),
            pltpu.VMEM((3 * ch, 9 * ch), BF16),
            pltpu.VMEM((3 * ch, 9 * ch), BF16),
            pltpu.VMEM((2 * ch, flat + 2 * hy), BF16),
            pltpu.VMEM((ch, flat + 2 * hy), BF16),
            pltpu.VMEM((ch, flat + 2 * hy), BF16),
            pltpu.VMEM((9 * ch, flat + 2 * hy), BF16),
            pltpu.VMEM((9 * ch, flat + 2 * hy), BF16),
            pltpu.VMEM((3 * ch, flat + 2 * hy), BF16),
            pltpu.VMEM((2, n_a, 8, ch), F32),
            pltpu.VMEM((2, n_b, 8, ch), F32),
            pltpu.VMEM((2, rows, LANES), F32),
            pltpu.VMEM((2, rows // 2, LANES), F32),
            pltpu.VMEM((2, rows // 2, LANES), F32),
            pltpu.VMEM((2, n_dp - 1, c_a, LANES), F32),
            pltpu.VMEM((2, c_a, LANES), F32),
            pltpu.VMEM((2, n_b - 1, c_b, LANES), F32),
            pltpu.VMEM((2, c_a, LANES), BF16),
            dma((3, 2)), dma((3, 2)),
            dma((2, n_a + n_b)), dma((2, n_a + n_b)),
            dma((2, 2 * (n_a + n_b))), dma((2, 2 * (n_a + n_b))),
        ],
        compiler_params=pltpu.CompilerParams(
            collective_id=0, has_side_effects=True, vmem_limit_bytes=48 * 2**20),
    )(
        xd, occupied[0], conv_one.reshape(27 * ch, ch), conv_two.reshape(27 * ch, ch),
        gain.reshape(1, ch), shift.reshape(1, ch),
    )
    planes = features.shape[1:]
    so, ig, g1, g2, gg, sg = pl.pallas_call(
        functools.partial(unpack, ch),
        out_shape=(
            jax.ShapeDtypeStruct(planes, BF16),
            jax.ShapeDtypeStruct(planes, BF16),
            jax.ShapeDtypeStruct((27 * ch, ch), F32),
            jax.ShapeDtypeStruct((27 * ch, ch), F32),
            jax.ShapeDtypeStruct((1, ch), F32),
            jax.ShapeDtypeStruct((1, ch), F32),
        ),
        in_specs=[vmem] * 4,
        out_specs=[vmem] * 6,
        compiler_params=pltpu.CompilerParams(vmem_limit_bytes=16 * 2**20),
    )(so.reshape(planes), ig.reshape(planes), q4, sums)
    shape = features.shape
    return (so.reshape(shape), ig.reshape(shape), g1.reshape(27, ch, ch),
            g2.reshape(27, ch, ch), gg.reshape(ch), sg.reshape(ch))


def solution(mesh):
    split = P("dp", None, "tile", None)
    return jax.shard_map(
        functools.partial(local, mesh.shape["dp"], mesh.shape["tile"]),
        mesh=mesh,
        in_specs=(split, P("dp", "tile", None), P(), P(), P(), P(), split),
        out_specs=(split, split, P(), P(), P(), P()),
        check_vma=False,
    )
```
